32 devices in a mesh: groups: 2 (over y), dp: 4 (over x, core), tensor: 4 (over z).
Axes of the slice: x: 2, y: 2, z: 4, core: 2. Of those that a mesh axis runs over, the one named last changes fastest.
Arguments:
- output_gradient: bfloat16 [4096, 8192], P(('groups', 'dp', 'tensor')), parts along dimension 0, may hold values from -6 to 6
- attention_input: bfloat16 [4096, 8192], P(('groups', 'dp'), 'tensor'), parts along dimension 0, may hold values from -6 to 6
- output_weight: bfloat16 [8192, 8192], P('tensor'), may hold values from -0.0625 to 0.0625
- adapter_down_weight: bfloat16 [16, 8192, 16], P('dp', 'tensor'), may hold values from -0.0625 to 0.0625
- adapter_up_weight: bfloat16 [16, 16, 8192], P('dp', None, 'tensor'), may hold values from -0.125 to 0.125
- tenant_of_block: int32 [32], P(('groups', 'dp')), parts along dimension 0, may hold values from 0 to 15
- slot_of_tenant: int32 [16], replicated, may hold values from 0 to 15, each once
Outputs:
- grad_in: bfloat16 [4096, 8192], P(('groups', 'dp'), 'tensor'), parts along dimension 0
- down_gradient: float32 [32, 8192, 16], P(('groups', 'dp'), 'tensor'), parts along dimension 0
- up_gradient: float32 [32, 16, 8192], P(('groups', 'dp'), None, 'tensor'), parts along dimension 0
The draws below stay inside these ranges and needn't reach their ends.
There are 2 independent parts, one for each index of `groups`. The reference program is written for one: setup_inputs(seed, part) draws one part's arguments, and reference() takes and returns one part's arrays. A program takes and returns all parts, laid end to end along the dimension named above; an argument that names none is the same for every part. Nothing has to cross between parts.
All inputs are finite; a program needn't handle non-finite values.
Results may differ from the reference program's by a relative error of at most 0.0034.
Values may be sent and summed in bfloat16 or wider, within the bound.
A program may use at most 128 MiB of HBM per device.

```python
import math
import jax
import jax.numpy as jnp
import numpy as np

MODEL_WIDTH = 8192
ADAPTER_RANK = 16
BLOCK = 128
TENANT_TOTAL = 16
ROWS = 2048


def set_ends(values, rng, smallest, top_value):
    longest = values.shape.index(max(values.shape))
    spots = []
    for shift in (0, 1):
        where = [jax.random.randint(jax.random.fold_in(rng, axis), (), 0, length) for axis, length in enumerate(values.shape)]
        where[longest] = (where[longest] + shift) % values.shape[longest]
        spots.append(tuple(where))
    return values.at[spots[0]].set(smallest).at[spots[1]].set(top_value)


def block_levels(rng, shape, split, least, top_value):
    def one(axis_at, blocks):
        steps = jax.random.uniform(jax.random.fold_in(jax.random.fold_in(rng, 6), axis_at), (blocks,), jnp.float32, least / len(split), top_value / len(split))
        return jnp.repeat(jnp.exp(steps), shape[axis_at] // blocks).reshape((-1,) + (1,) * (len(shape) - axis_at - 1))

    loudness = one(*split[0])
    for cut in split[1:]:
        loudness = loudness * one(*cut)
    return loudness


def rank_bounds(count, slope):
    weights = [(1 << 20) // math.isqrt(rank ** slope) + 1 for rank in range(1, count + 1)]
    scale = 1 + sum(weights) // (1 << 30)
    return np.cumsum(np.array([max(1, weight // scale) for weight in weights]))


def skewed_ids(rng, extent, count, slope):
    grid = rank_bounds(count, slope)
    pick = jax.random.randint(jax.random.fold_in(rng, 1), extent, 0, int(grid[count - 1]))
    standing = jnp.searchsorted(jnp.asarray(grid, jnp.int32), pick, side="right")
    return jax.random.permutation(jax.random.fold_in(rng, 2), count)[standing].astype(jnp.int32)


def noise(key, extent, scale, limit, split=(), held_as=jnp.bfloat16):
    result = jax.random.normal(key, extent, jnp.float32) * scale
    if len(split) > 0:
        result = block_levels(key, extent, split, -0.22, 0.18) * result
    return jnp.clip(result, min=-limit, max=limit).astype(held_as)


def setup_inputs(seed: int = 0, part: int = 0) -> dict:
    streams_of = jax.random.split(jax.random.key(seed), 8)
    part_keys = jax.random.split(jax.random.fold_in(streams_of[7], part), 8)
    return {
        "output_gradient": noise(part_keys[0], (ROWS, MODEL_WIDTH), 1.0, 6.0, ((0, 16),)),
        "attention_input": noise(part_keys[1], (ROWS, MODEL_WIDTH), 1.0, 6.0, ((0, 4), (1, 4))),
        "output_weight": noise(streams_of[2], (MODEL_WIDTH, MODEL_WIDTH), MODEL_WIDTH ** -0.5, 0.0625, ((0, 4),)),
        "adapter_down_weight": noise(streams_of[3], (TENANT_TOTAL, MODEL_WIDTH, ADAPTER_RANK), MODEL_WIDTH ** -0.5, 0.0625, ((0, 4), (1, 4))),
        "adapter_up_weight": noise(streams_of[4], (TENANT_TOTAL, ADAPTER_RANK, MODEL_WIDTH), (MODEL_WIDTH // 4) ** -0.5, 0.125, ((0, 4), (2, 4))),
        "tenant_of_block": set_ends(skewed_ids(part_keys[5], (ROWS // BLOCK,), TENANT_TOTAL, 2), jax.random.fold_in(part_keys[5], 3), 0, TENANT_TOTAL - 1).astype(jnp.int32),
        "slot_of_tenant": jax.random.permutation(streams_of[6], TENANT_TOTAL).astype(jnp.int32),
    }


adapter_scale = 2.0


def reference(output_gradient, attention_input, output_weight, adapter_down_weight, adapter_up_weight, tenant_of_block, slot_of_tenant):
    slot_of_block = jnp.take(slot_of_tenant, tenant_of_block).astype(jnp.int32)
    block_count = tenant_of_block.shape[0]
    width = output_gradient.shape[1]
    dy_blocks = output_gradient.reshape(block_count, BLOCK, width).astype(jnp.float32)
    in_blocks = attention_input.reshape(block_count, BLOCK, width).astype(jnp.float32)
    selected_down = jnp.take(adapter_down_weight, slot_of_block, axis=0).astype(jnp.float32)
    selected_up = jnp.take(adapter_up_weight, slot_of_block, axis=0).astype(jnp.float32)
    up_activation = jnp.einsum("bnc,brc->bnr", dy_blocks, selected_up)
    down_activation = jnp.einsum("bnd,bdr->bnr", in_blocks, selected_down)
    scaled_up_result = (adapter_scale * up_activation).astype(jnp.bfloat16)
    scaled_down_result = (adapter_scale * down_activation).astype(jnp.bfloat16)
    base_part = jnp.dot(output_gradient, output_weight.T, preferred_element_type=jnp.float32)
    extra = jnp.einsum("bnr,bdr->bnd", scaled_up_result.astype(jnp.float32), selected_down)
    grad_in = (base_part + extra.reshape(base_part.shape)).astype(jnp.bfloat16)
    down_by_block = jnp.einsum("bnd,bnr->bdr", in_blocks, scaled_up_result.astype(jnp.float32))
    up_by_block = jnp.einsum("bnr,bnc->brc", scaled_down_result.astype(jnp.float32), dy_blocks)
    down_gradient = jnp.zeros(adapter_down_weight.shape, jnp.float32).at[slot_of_block].add(down_by_block)
    up_gradient = jnp.zeros(adapter_up_weight.shape, jnp.float32).at[slot_of_block].add(up_by_block)
    return grad_in, down_gradient, up_gradient
```

```python
import jax
import jax.numpy as jnp
from jax import lax
from jax.sharding import PartitionSpec as P

adapter_scale = 2.0
column_chunks = 2


def body(
    tensor_size,
    output_gradient,
    attention_input,
    output_weight,
    adapter_down_weight,
    adapter_up_weight,
    tenant_of_block,
    slot_of_tenant,
):
    f32, bf16 = jnp.float32, jnp.bfloat16
    n = tensor_size
    me = lax.axis_index("tensor")
    block_count = tenant_of_block.shape[0]
    shard_rows, local_width = attention_input.shape
    own_rows, width = output_gradient.shape
    rows_per_block = shard_rows // block_count
    held = adapter_down_weight.shape[0]
    rank = adapter_down_weight.shape[2]
    owners_per_block = n // block_count
    chunk = width // column_chunks

    right = [(i, i + 1) for i in range(n - 1)]
    left = [(i + 1, i) for i in range(n - 1)]
    pieces = [output_gradient[:, c * chunk : (c + 1) * chunk] for c in range(column_chunks)]
    weights = [output_weight[:, c * chunk : (c + 1) * chunk] for c in range(column_chunks)]
    from_left, from_right = [pieces], [pieces]
    for s in range(n - 1):
        from_left.append([lax.ppermute(p, "tensor", right) for p in from_left[-1]])
        from_right.append([lax.ppermute(p, "tensor", left) for p in from_right[-1]])

    slot_of_block = jnp.take(slot_of_tenant, tenant_of_block)
    every_slot = lax.all_gather(slot_of_block, "dp", axis=0, tiled=True)
    both = jnp.concatenate([jnp.swapaxes(adapter_down_weight, 1, 2), adapter_up_weight], axis=1)
    both_all = lax.all_gather(both, "dp", axis=0, tiled=True)
    selected = jnp.take(both_all, slot_of_block, axis=0)
    selected_down = selected[:, :rank]
    selected_up = selected[:, rank:]

    up_pieces = jnp.repeat(selected_up, owners_per_block, axis=0)
    up_own = lax.all_to_all(up_pieces, "tensor", 0, 0, tiled=True)
    gradient_parts = output_gradient.reshape(own_rows, n, local_width)
    up_act = jnp.einsum("ntc,trc->nr", gradient_parts, up_own, preferred_element_type=f32)
    up_scaled_own = (adapter_scale * up_act).astype(bf16)
    up_scaled = lax.all_gather(up_scaled_own, "tensor", axis=0, tiled=True)
    up_blocks = up_scaled.reshape(block_count, rows_per_block, rank)

    in_blocks = attention_input.reshape(block_count, rows_per_block, local_width)
    down_part = jnp.einsum("bnd,brd->bnr", in_blocks, selected_down, preferred_element_type=f32)
    down_pieces = lax.all_to_all(down_part.reshape(n, own_rows * rank), "tensor", 0, 0, tiled=True)
    down_act = jnp.sum(down_pieces, axis=0).reshape(own_rows, rank)
    down_scaled = (adapter_scale * down_act).astype(bf16)

    up_outer = jnp.einsum("nr,ntc->trc", down_scaled, gradient_parts, preferred_element_type=f32)
    up_shared = lax.all_to_all(up_outer.astype(bf16), "tensor", 0, 0, tiled=True)
    up_by_block = jnp.sum(
        up_shared.astype(f32).reshape(block_count, owners_per_block, rank, local_width), axis=1
    )
    down_by_block = jnp.einsum("bnr,bnd->brd", up_blocks, in_blocks, preferred_element_type=f32)
    grads = jnp.concatenate([down_by_block.astype(bf16), up_by_block.astype(bf16)], axis=1)
    every_grad = lax.all_gather(grads, "dp", axis=0, tiled=True)
    my_slots = lax.axis_index("dp") * held + jnp.arange(held, dtype=jnp.int32)
    selector = (my_slots[:, None] == every_slot[None, :]).astype(bf16)
    summed = jnp.einsum("sb,bkc->skc", selector, every_grad, preferred_element_type=f32)
    down_gradient = jnp.swapaxes(summed[:, :rank], 1, 2)
    up_gradient = summed[:, rank:]

    extra = jnp.einsum("bnr,brd->bnd", up_blocks, selected_down, preferred_element_type=f32)
    extra = extra.reshape(shard_rows, local_width)

    def extra_of(owner):
        return lax.dynamic_slice_in_dim(extra, owner * own_rows, own_rows, 0)

    def product(parts, added):
        total = added
        for p, w in zip(parts, weights):
            total = total + jnp.einsum("kd,hd->kh", p, w, preferred_element_type=f32)
        return total.astype(bf16)

    grad_in = jnp.zeros((shard_rows, local_width), bf16)
    grad_in = lax.dynamic_update_slice_in_dim(
        grad_in, product(pieces, extra_of(me)), me * own_rows, 0
    )
    for s in range(n - 1):
        left_owner, right_owner = lax.rem(me + n - 1 - s, n), lax.rem(me + 1 + s, n)
        if s + 1 <= n - 2 - s:
            parts = [
                jnp.concatenate([a, b], axis=0)
                for a, b in zip(from_left[s + 1], from_right[s + 1])
            ]
            result = product(
                parts, jnp.concatenate([extra_of(left_owner), extra_of(right_owner)], axis=0)
            )
            for k, owner in enumerate((left_owner, right_owner)):
                valid = me >= s + 1 if k == 0 else me <= n - 2 - s
                old = lax.dynamic_slice_in_dim(grad_in, owner * own_rows, own_rows, 0)
                new = result[k * own_rows : (k + 1) * own_rows]
                grad_in = lax.dynamic_update_slice_in_dim(
                    grad_in, jnp.where(valid, new, old), owner * own_rows, 0
                )
        else:
            use_left = me >= s + 1
            owner = jnp.where(use_left, left_owner, right_owner)
            parts = [
                jnp.where(use_left, a, b) for a, b in zip(from_left[s + 1], from_right[s + 1])
            ]
            result = product(parts, extra_of(owner))
            valid = use_left | (me <= n - 2 - s)
            old = lax.dynamic_slice_in_dim(grad_in, owner * own_rows, own_rows, 0)
            grad_in = lax.dynamic_update_slice_in_dim(
                grad_in, jnp.where(valid, result, old), owner * own_rows, 0
            )
    return grad_in, down_gradient, up_gradient


def solution(mesh):
    in_specs = (
        P(("groups", "dp", "tensor"), None),
        P(("groups", "dp"), "tensor"),
        P("tensor", None),
        P("dp", "tensor", None),
        P("dp", None, "tensor"),
        P(("groups", "dp")),
        P(),
    )
    out_specs = (
        P(("groups", "dp"), "tensor"),
        P(("groups", "dp"), "tensor", None),
        P(("groups", "dp"), None, "tensor"),
    )
    n = mesh.shape["tensor"]

    def per_device(*args):
        return body(n, *args)

    return jax.shard_map(per_device, mesh=mesh, in_specs=in_specs, out_specs=out_specs, check_vma=False)
```

```python
import functools

import jax
import jax.numpy as jnp
from jax import lax
from jax.experimental import pallas as pl
from jax.experimental.pallas import tpu as pltpu
from jax.sharding import PartitionSpec as P

adapter_scale = 2.0
MESH = pl.DeviceIdType.MESH
NT = (((1,), (1,)), ((), ()))
NN = (((1,), (0,)), ((), ()))
TN = (((0,), (0,)), ((), ()))


def dot(a, b, dims):
    return lax.dot_general(a, b, dims, preferred_element_type=jnp.float32)


def kernel(
    n,
    dp,
    chunks,
    slots_ref,
    pick_ref,
    adapters_ref,
    dy_ref,
    x_ref,
    w_ref,
    out_ref,
    grads_ref,
    w_v,
    rows_v,
    acc,
    x_v,
    all_adapters,
    selected,
    up_own,
    down_send,
    down_recv,
    ups,
    outer_send,
    outer_recv,
    by_block,
    share_send,
    share_recv,
    total,
    out_v,
    w_sem,
    x_sem,
    dy_sem,
    hop_send,
    hop_recv,
    a_send,
    a_recv,
    z_send,
    z_recv,
    s_send,
    s_recv,
    out_sem,
    grads_sem,
):
    f32, bf16 = jnp.float32, jnp.bfloat16
    me, me_dp = lax.axis_index("tensor"), lax.axis_index("dp")
    own_rows = dy_ref.shape[0]
    shard_rows, local = x_ref.shape
    chunk = dy_ref.shape[1] // chunks
    held, rank = adapters_ref.shape[0], adapters_ref.shape[1] // 2
    blocks = slots_ref.shape[0]
    per_block = n // blocks

    dy_in = [
        pltpu.make_async_copy(dy_ref.at[:, pl.ds(c * chunk, chunk)], rows_v.at[me, c], dy_sem.at[c])
        for c in range(chunks)
    ]
    for copy in dy_in:
        copy.start()
    x_in = pltpu.make_async_copy(x_ref, x_v, x_sem)
    x_in.start()
    w_in = [
        pltpu.make_async_copy(w_ref.at[:, pl.ds(c * chunk, chunk)], w_v.at[c], w_sem.at[c])
        for c in range(chunks)
    ]
    for copy in w_in:
        copy.start()

    barrier = pltpu.get_barrier_semaphore()
    for k in range(1, n):
        pl.semaphore_signal(
            barrier, inc=1, device_id={"tensor": lax.rem(me + k, n)}, device_id_type=MESH
        )
    for k in range(1, dp):
        pl.semaphore_signal(
            barrier, inc=1, device_id={"dp": lax.rem(me_dp + k, dp)}, device_id_type=MESH
        )
    pl.semaphore_wait(barrier, n - 1 + dp - 1)

    def hop(way, step, c):
        shard = jnp.clip(me - step if way == 0 else me + step, 0, n - 1)
        to = jnp.minimum(me + 1, n - 1) if way == 0 else jnp.maximum(me - 1, 0)
        return pltpu.make_async_remote_copy(
            src_ref=rows_v.at[shard, c],
            dst_ref=rows_v.at[shard, c],
            send_sem=hop_send.at[way, step, c],
            recv_sem=hop_recv.at[way, step, c],
            device_id={"tensor": to},
            device_id_type=MESH,
        )

    def sends(way, step):
        return (me >= step) & (me < n - 1) if way == 0 else (me + step <= n - 1) & (me > 0)

    def receives(way, step):
        return me >= step + 1 if way == 0 else me + step + 1 <= n - 1

    def incoming(way, step):
        return jnp.clip(me - 1 - step if way == 0 else me + 1 + step, 0, n - 1)

    def arrived(way, step, c):
        shard = incoming(way, step)
        return pltpu.make_async_remote_copy(
            src_ref=rows_v.at[shard, c],
            dst_ref=rows_v.at[shard, c],
            send_sem=hop_send.at[way, step, c],
            recv_sem=hop_recv.at[way, step, c],
            device_id={"tensor": jnp.minimum(me + 1, n - 1) if way == 0 else jnp.maximum(me - 1, 0)},
            device_id_type=MESH,
        )

    for c in range(chunks):
        dy_in[c].wait()
        for way in range(2):

            @pl.when(sends(way, 0))
            def _(way=way, c=c):
                hop(way, 0, c).start()

    def adapters_copy(k):
        peer = lax.rem(me_dp + k, dp)
        return pltpu.make_async_remote_copy(
            src_ref=adapters_ref,
            dst_ref=all_adapters.at[pl.ds(me_dp * held, held)],
            send_sem=a_send.at[k - 1],
            recv_sem=a_recv.at[k - 1],
            device_id={"dp": peer},
            device_id_type=MESH,
        )

    def adapters_arrival(k):
        source = lax.rem(me_dp + dp - k, dp)
        return pltpu.make_async_remote_copy(
            src_ref=adapters_ref,
            dst_ref=all_adapters.at[pl.ds(source * held, held)],
            send_sem=a_send.at[k - 1],
            recv_sem=a_recv.at[k - 1],
            device_id={"dp": source},
            device_id_type=MESH,
        )

    for k in range(1, dp):
        adapters_copy(k).start()
    all_adapters[pl.ds(me_dp * held, held)] = adapters_ref[...]

    def z_copy(kind, k, arrival=False):
        peer = lax.rem(me + (n - k if arrival else k), n)
        slot = peer if arrival else me
        source, target = {
            0: (lambda p: selected.at[p // per_block, pl.ds(rank, rank)], up_own),
            1: (lambda p: down_send.at[p], down_recv),
            2: (lambda p: ups.at[me], ups),
            3: (lambda p: outer_send.at[p], outer_recv),
        }[kind]
        return pltpu.make_async_remote_copy(
            src_ref=source(peer),
            dst_ref=target.at[slot],
            send_sem=z_send.at[kind, k - 1],
            recv_sem=z_recv.at[kind, k - 1],
            device_id={"tensor": peer},
            device_id_type=MESH,
        )

    def z_start(kind):
        for k in range(1, n):
            z_copy(kind, k).start()

    def z_wait(kind):
        for k in range(1, n):
            z_copy(kind, k, True).wait_recv()

    def share_copy(k, arrival=False):
        peer = lax.rem(me_dp + (dp - k if arrival else k), dp)
        return pltpu.make_async_remote_copy(
            src_ref=share_send.at[peer],
            dst_ref=share_recv.at[peer if arrival else me_dp],
            send_sem=s_send.at[k - 1],
            recv_sem=s_recv.at[k - 1],
            device_id={"dp": peer},
            device_id_type=MESH,
        )

    def own_features(t):
        return t * local // chunk, pl.ds(t * local % chunk, local)

    def select():
        for k in range(1, dp):
            adapters_arrival(k).wait_recv()
        for b in range(blocks):
            selected[b] = all_adapters[slots_ref[b]]
        z_start(0)
        x_in.wait()
        for t in range(n):
            down_send[t] = dot(
                selected[t // per_block, 0:rank], x_v[t * own_rows : (t + 1) * own_rows, :], NT
            )
        z_start(1)

    def activations():
        z_wait(0)
        z_wait(1)
        up_own[me] = selected[me // per_block, pl.ds(rank, rank)]
        down_recv[me] = down_send[me]
        up = jnp.zeros((rank, own_rows), f32)
        down = jnp.zeros((rank, own_rows), f32)
        for t in range(n):
            c, columns = own_features(t)
            up = up + dot(up_own[t], rows_v[me, c, :, columns], NT)
            down = down + down_recv[t]
        ups[me] = (adapter_scale * up).astype(bf16)
        z_start(2)
        down = (adapter_scale * down).astype(bf16)
        for t in range(n):
            c, columns = own_features(t)
            outer_send[t] = dot(down, rows_v[me, c, :, columns], NN).astype(bf16)
        z_start(3)

    def gradients():
        z_wait(2)
        z_wait(3)
        outer_recv[me] = outer_send[me]
        for b in range(blocks):
            down_sum = jnp.zeros((rank, local), f32)
            up_sum = jnp.zeros((rank, local), f32)
            for t in range(b * per_block, (b + 1) * per_block):
                down_sum = down_sum + dot(ups[t], x_v[t * own_rows : (t + 1) * own_rows, :], NN)
                up_sum = up_sum + outer_recv[t].astype(f32)
            by_block[b, 0:rank] = down_sum
            by_block[b, rank : 2 * rank] = up_sum

        def share(slot):
            value = pick_ref[slot, 0] * by_block[0]
            for b in range(1, blocks):
                value = value + pick_ref[slot, b] * by_block[b]
            return value

        for k in range(1, dp):
            peer = lax.rem(me_dp + k, dp)
            for s in range(held):
                share_send[peer, s] = share(peer * held + s).astype(bf16)
            share_copy(k).start()
        for s in range(held):
            total[s] = share(me_dp * held + s)
        for t in range(n):
            acc[t] += dot(ups[t], selected[t // per_block, 0:rank], TN)

    def owners():
        for k in range(1, dp):
            share_copy(k, True).wait_recv()
            source = lax.rem(me_dp + dp - k, dp)
            for s in range(held):
                total[s] += share_recv[source, s].astype(f32)
        pltpu.make_async_copy(total, grads_ref, grads_sem).start()

    tile = min(512, local)

    def multiply(shard, c):
        @pl.loop(0, local // tile)
        def _(i):
            at = pl.ds(pl.multiple_of(i * tile, tile), tile)
            acc[shard, :, at] += dot(rows_v[shard, c], w_v[c, at, :], NT)

    def out_copy(shard):
        return pltpu.make_async_copy(
            out_v.at[shard], out_ref.at[pl.ds(shard * own_rows, own_rows)], out_sem.at[shard]
        )

    def finish(shard):
        out_v[shard] = acc[shard].astype(bf16)
        out_copy(shard).start()

    acc[...] = jnp.zeros_like(acc)
    for c in range(chunks):
        w_in[c].wait()
        multiply(me, c)

    phases = {1: select, 3: activations, 5: gradients, 9: owners}
    ready, waiting, event = False, [(None, None)], 0
    last_phase = 9

    def flush(items):
        for way, step in items:
            if way is None:
                finish(me)
            else:

                @pl.when(receives(way, step))
                def _(way=way, step=step):
                    finish(incoming(way, step))

    for step in range(n - 1):
        for c in range(chunks):
            for way in range(2):

                @pl.when(receives(way, step))
                def _(way=way, step=step, c=c):
                    arrived(way, step, c).wait_recv()
                    if step + 1 < n - 1:

                        @pl.when(sends(way, step + 1))
                        def _():
                            hop(way, step + 1, c).start()

            for way in range(2):

                @pl.when(receives(way, step))
                def _(way=way, step=step, c=c):
                    multiply(incoming(way, step), c)

            if event in phases:
                phases[event]()
                if event == 5:
                    ready = True
            event += 1
        waiting += [(0, step), (1, step)]
        if ready:
            flush(waiting)
            waiting = []
    for step in range(n - 1):
        for way in range(2):
            for c in range(chunks):

                @pl.when(sends(way, step))
                def _(way=way, step=step, c=c):
                    hop(way, step, c).wait_send()

    for k in range(1, dp):
        adapters_copy(k).wait_send()
        share_copy(k).wait_send()
    for kind in range(4):
        for k in range(1, n):
            z_copy(kind, k).wait_send()
    pltpu.make_async_copy(total, grads_ref, grads_sem).wait()
    for t in range(n):
        out_copy(t).wait()


def body(
    n,
    dp,
    output_gradient,
    attention_input,
    output_weight,
    adapter_down_weight,
    adapter_up_weight,
    tenant_of_block,
    slot_of_tenant,
):
    f32, bf16 = jnp.float32, jnp.bfloat16
    blocks = tenant_of_block.shape[0]
    shard_rows, local = attention_input.shape
    own_rows, width = output_gradient.shape
    held, _, rank = adapter_down_weight.shape
    chunks = max(1, own_rows // 32)
    chunk = width // chunks

    slots = jnp.take(slot_of_tenant, tenant_of_block)
    pick = (jnp.arange(dp * held, dtype=jnp.int32)[:, None] == slots[None, :]).astype(f32)
    adapters = jnp.concatenate([jnp.swapaxes(adapter_down_weight, 1, 2), adapter_up_weight], axis=1)
    dma = pltpu.SemaphoreType.DMA
    smem = pl.BlockSpec(memory_space=pltpu.SMEM)
    vmem = pl.BlockSpec(memory_space=pltpu.VMEM)
    anywhere = pl.BlockSpec(memory_space=pl.ANY)
    grad_in, grads = pl.pallas_call(
        functools.partial(kernel, n, dp, chunks),
        out_shape=(
            jax.ShapeDtypeStruct((shard_rows, local), bf16),
            jax.ShapeDtypeStruct((held, 2 * rank, local), f32),
        ),
        in_specs=[smem, smem, vmem, anywhere, anywhere, anywhere],
        out_specs=(anywhere, anywhere),
        scratch_shapes=[
            pltpu.VMEM((chunks, local, chunk), bf16),
            pltpu.VMEM((n, chunks, own_rows, chunk), bf16),
            pltpu.VMEM((n, own_rows, local), f32),
            pltpu.VMEM((shard_rows, local), bf16),
            pltpu.VMEM((dp * held, 2 * rank, local), bf16),
            pltpu.VMEM((blocks, 2 * rank, local), bf16),
            pltpu.VMEM((n, rank, local), bf16),
            pltpu.VMEM((n, rank, own_rows), f32),
            pltpu.VMEM((n, rank, own_rows), f32),
            pltpu.VMEM((n, rank, own_rows), bf16),
            pltpu.VMEM((n, rank, local), bf16),
            pltpu.VMEM((n, rank, local), bf16),
            pltpu.VMEM((blocks, 2 * rank, local), f32),
            pltpu.VMEM((dp, held, 2 * rank, local), bf16),
            pltpu.VMEM((dp, held, 2 * rank, local), bf16),
            pltpu.VMEM((held, 2 * rank, local), f32),
            pltpu.VMEM((n, own_rows, local), bf16),
            dma((chunks,)),
            dma,
            dma((chunks,)),
            dma((2, n - 1, chunks)),
            dma((2, n - 1, chunks)),
            dma((dp - 1,)),
            dma((dp - 1,)),
            dma((4, n - 1)),
            dma((4, n - 1)),
            dma((dp - 1,)),
            dma((dp - 1,)),
            dma((n,)),
            dma,
        ],
        compiler_params=pltpu.CompilerParams(
            collective_id=0, has_side_effects=True, vmem_limit_bytes=62 * 1024 * 1024
        ),
        cost_estimate=pl.CostEstimate(
            flops=2 * shard_rows * width * local,
            bytes_accessed=2 * local * width,
            transcendentals=0,
        ),
        name="gather_and_multiply",
    )(slots, pick, adapters, output_gradient, attention_input, output_weight)
    return grad_in, jnp.swapaxes(grads[:, :rank], 1, 2), grads[:, rank:]


def solution(mesh):
    in_specs = (
        P(("groups", "dp", "tensor"), None),
        P(("groups", "dp"), "tensor"),
        P("tensor", None),
        P("dp", "tensor", None),
        P("dp", None, "tensor"),
        P(("groups", "dp")),
        P(),
    )
    out_specs = (
        P(("groups", "dp"), "tensor"),
        P(("groups", "dp"), "tensor", None),
        P(("groups", "dp"), None, "tensor"),
    )
    sizes = mesh.shape["tensor"], mesh.shape["dp"]

    def per_device(*args):
        return body(*sizes, *args)

    return jax.shard_map(per_device, mesh=mesh, in_specs=in_specs, out_specs=out_specs, check_vma=False)
```

```python
import functools

import jax
import jax.numpy as jnp
from jax import lax
from jax.experimental import pallas as pl
from jax.experimental.pallas import tpu as pltpu
from jax.sharding import PartitionSpec as P

adapter_scale = 2.0
MESH = pl.DeviceIdType.MESH
NT = (((1,), (1,)), ((), ()))
NN = (((1,), (0,)), ((), ()))
TN = (((0,), (0,)), ((), ()))


def dot(a, b, dims):
    return lax.dot_general(a, b, dims, preferred_element_type=jnp.float32)


def kernel(
    n,
    dp,
    chunks,
    tenant_ref,
    slot_ref,
    adapters_ref,
    dy_ref,
    x_ref,
    w_ref,
    out_ref,
    grads_ref,
    w_v,
    rows_v,
    acc,
    x_v,
    all_adapters,
    selected,
    up_own,
    down_send,
    down_recv,
    ups,
    outer_send,
    outer_recv,
    by_block,
    share_send,
    share_recv,
    total,
    out_v,
    w_sem,
    x_sem,
    dy_sem,
    hop_send,
    hop_recv,
    a_send,
    a_recv,
    z_send,
    z_recv,
    s_send,
    s_recv,
    out_sem,
    grads_sem,
):
    f32, bf16 = jnp.float32, jnp.bfloat16
    me, me_dp = lax.axis_index("tensor"), lax.axis_index("dp")
    own_rows = dy_ref.shape[0]
    shard_rows, local = x_ref.shape
    chunk = dy_ref.shape[1] // chunks
    held, rank = adapters_ref.shape[0], adapters_ref.shape[1] // 2
    blocks = tenant_ref.shape[0]
    per_block = n // blocks
    slots = [slot_ref[tenant_ref[b]] for b in range(blocks)]

    dy_in = [
        pltpu.make_async_copy(dy_ref.at[:, pl.ds(c * chunk, chunk)], rows_v.at[me, c], dy_sem.at[c])
        for c in range(chunks)
    ]
    for copy in dy_in:
        copy.start()
    x_in = pltpu.make_async_copy(x_ref, x_v, x_sem)
    x_in.start()
    w_in = [
        pltpu.make_async_copy(w_ref.at[:, pl.ds(c * chunk, chunk)], w_v.at[c], w_sem.at[c])
        for c in range(chunks)
    ]
    for copy in w_in:
        copy.start()

    barrier = pltpu.get_barrier_semaphore()
    for k in range(1, n):
        pl.semaphore_signal(
            barrier, inc=1, device_id={"tensor": lax.rem(me + k, n)}, device_id_type=MESH
        )
    for k in range(1, dp):
        pl.semaphore_signal(
            barrier, inc=1, device_id={"dp": lax.rem(me_dp + k, dp)}, device_id_type=MESH
        )
    pl.semaphore_wait(barrier, n - 1 + dp - 1)

    def hop(way, step, c):
        shard = jnp.clip(me - step if way == 0 else me + step, 0, n - 1)
        to = jnp.minimum(me + 1, n - 1) if way == 0 else jnp.maximum(me - 1, 0)
        return pltpu.make_async_remote_copy(
            src_ref=rows_v.at[shard, c],
            dst_ref=rows_v.at[shard, c],
            send_sem=hop_send.at[way, step, c],
            recv_sem=hop_recv.at[way, step, c],
            device_id={"tensor": to},
            device_id_type=MESH,
        )

    def sends(way, step):
        return (me >= step) & (me < n - 1) if way == 0 else (me + step <= n - 1) & (me > 0)

    def receives(way, step):
        return me >= step + 1 if way == 0 else me + step + 1 <= n - 1

    def incoming(way, step):
        return jnp.clip(me - 1 - step if way == 0 else me + 1 + step, 0, n - 1)

    def arrived(way, step, c):
        shard = incoming(way, step)
        return pltpu.make_async_remote_copy(
            src_ref=rows_v.at[shard, c],
            dst_ref=rows_v.at[shard, c],
            send_sem=hop_send.at[way, step, c],
            recv_sem=hop_recv.at[way, step, c],
            device_id={"tensor": jnp.minimum(me + 1, n - 1) if way == 0 else jnp.maximum(me - 1, 0)},
            device_id_type=MESH,
        )

    for c in range(chunks):
        dy_in[c].wait()
        for way in range(2):

            @pl.when(sends(way, 0))
            def _(way=way, c=c):
                hop(way, 0, c).start()

    def adapters_copy(k):
        peer = lax.rem(me_dp + k, dp)
        return pltpu.make_async_remote_copy(
            src_ref=adapters_ref,
            dst_ref=all_adapters.at[pl.ds(me_dp * held, held)],
            send_sem=a_send.at[k - 1],
            recv_sem=a_recv.at[k - 1],
            device_id={"dp": peer},
            device_id_type=MESH,
        )

    def adapters_arrival(k):
        source = lax.rem(me_dp + dp - k, dp)
        return pltpu.make_async_remote_copy(
            src_ref=adapters_ref,
            dst_ref=all_adapters.at[pl.ds(source * held, held)],
            send_sem=a_send.at[k - 1],
            recv_sem=a_recv.at[k - 1],
            device_id={"dp": source},
            device_id_type=MESH,
        )

    for k in range(1, dp):
        adapters_copy(k).start()
    all_adapters[pl.ds(me_dp * held, held)] = adapters_ref[...]

    def z_copy(kind, k, arrival=False):
        peer = lax.rem(me + (n - k if arrival else k), n)
        slot = peer if arrival else me
        source, target = {
            0: (lambda p: selected.at[p // per_block, pl.ds(rank, rank)], up_own),
            1: (lambda p: down_send.at[p], down_recv),
            2: (lambda p: ups.at[me], ups),
            3: (lambda p: outer_send.at[p], outer_recv),
        }[kind]
        return pltpu.make_async_remote_copy(
            src_ref=source(peer),
            dst_ref=target.at[slot],
            send_sem=z_send.at[kind, k - 1],
            recv_sem=z_recv.at[kind, k - 1],
            device_id={"tensor": peer},
            device_id_type=MESH,
        )

    def z_start(kind):
        for k in range(1, n):
            z_copy(kind, k).start()

    def z_wait(kind):
        for k in range(1, n):
            z_copy(kind, k, True).wait_recv()

    def share_copy(k, arrival=False):
        peer = lax.rem(me_dp + (dp - k if arrival else k), dp)
        return pltpu.make_async_remote_copy(
            src_ref=share_send.at[peer],
            dst_ref=share_recv.at[peer if arrival else me_dp],
            send_sem=s_send.at[k - 1],
            recv_sem=s_recv.at[k - 1],
            device_id={"dp": peer},
            device_id_type=MESH,
        )

    def own_features(t):
        return t * local // chunk, pl.ds(t * local % chunk, local)

    def select():
        for k in range(1, dp):
            adapters_arrival(k).wait_recv()
        for b in range(blocks):
            selected[b] = all_adapters[slots[b]]
        z_start(0)
        x_in.wait()
        for t in range(n):
            down_send[t] = dot(
                selected[t // per_block, 0:rank], x_v[t * own_rows : (t + 1) * own_rows, :], NT
            )
        z_start(1)

    def activations():
        z_wait(0)
        z_wait(1)
        up_own[me] = selected[me // per_block, pl.ds(rank, rank)]
        down_recv[me] = down_send[me]
        up = jnp.zeros((rank, own_rows), f32)
        down = jnp.zeros((rank, own_rows), f32)
        for t in range(n):
            c, columns = own_features(t)
            up = up + dot(up_own[t], rows_v[me, c, :, columns], NT)
            down = down + down_recv[t]
        ups[me] = (adapter_scale * up).astype(bf16)
        z_start(2)
        down = (adapter_scale * down).astype(bf16)
        for t in range(n):
            c, columns = own_features(t)
            outer_send[t] = dot(down, rows_v[me, c, :, columns], NN).astype(bf16)
        z_start(3)

    def gradients():
        z_wait(2)
        z_wait(3)
        outer_recv[me] = outer_send[me]
        for b in range(blocks):
            down_sum = jnp.zeros((rank, local), f32)
            up_sum = jnp.zeros((rank, local), f32)
            for t in range(b * per_block, (b + 1) * per_block):
                down_sum = down_sum + dot(ups[t], x_v[t * own_rows : (t + 1) * own_rows, :], NN)
                up_sum = up_sum + outer_recv[t].astype(f32)
            by_block[b, 0:rank] = down_sum
            by_block[b, rank : 2 * rank] = up_sum

        def share(slot):
            value = jnp.zeros((2 * rank, local), f32)
            for b in range(blocks):
                value = value + (slots[b] == slot).astype(f32) * by_block[b]
            return value

        for k in range(1, dp):
            peer = lax.rem(me_dp + k, dp)
            for s in range(held):
                share_send[peer, s] = share(peer * held + s).astype(bf16)
            share_copy(k).start()
        for s in range(held):
            total[s] = share(me_dp * held + s)
        for t in range(n):
            acc[t] += dot(ups[t], selected[t // per_block, 0:rank], TN)

    def owners():
        for k in range(1, dp):
            share_copy(k, True).wait_recv()
            source = lax.rem(me_dp + dp - k, dp)
            for s in range(held):
                total[s] += share_recv[source, s].astype(f32)
        pltpu.make_async_copy(total, grads_ref, grads_sem).start()

    tile = min(512, local)

    def multiply(shard, c):
        @pl.loop(0, local // tile)
        def _(i):
            at = pl.ds(pl.multiple_of(i * tile, tile), tile)
            acc[shard, :, at] += dot(rows_v[shard, c], w_v[c, at, :], NT)

    def out_copy(shard):
        return pltpu.make_async_copy(
            out_v.at[shard], out_ref.at[pl.ds(shard * own_rows, own_rows)], out_sem.at[shard]
        )

    def finish(shard):
        out_v[shard] = acc[shard].astype(bf16)
        out_copy(shard).start()

    acc[...] = jnp.zeros_like(acc)
    for c in range(chunks):
        w_in[c].wait()
        multiply(me, c)

    phases = {1: select, 3: activations, 5: gradients, 9: owners}
    ready, waiting, event = False, [(None, None)], 0
    last_phase = 9

    def flush(items):
        for way, step in items:
            if way is None:
                finish(me)
            else:

                @pl.when(receives(way, step))
                def _(way=way, step=step):
                    finish(incoming(way, step))

    for step in range(n - 1):
        for c in range(chunks):
            for way in range(2):

                @pl.when(receives(way, step))
                def _(way=way, step=step, c=c):
                    arrived(way, step, c).wait_recv()
                    if step + 1 < n - 1:

                        @pl.when(sends(way, step + 1))
                        def _():
                            hop(way, step + 1, c).start()

            for way in range(2):

                @pl.when(receives(way, step))
                def _(way=way, step=step, c=c):
                    multiply(incoming(way, step), c)

            if event in phases:
                phases[event]()
                if event == 5:
                    ready = True
            event += 1
        waiting += [(0, step), (1, step)]
        if ready:
            flush(waiting)
            waiting = []
    for step in range(n - 1):
        for way in range(2):
            for c in range(chunks):

                @pl.when(sends(way, step))
                def _(way=way, step=step, c=c):
                    hop(way, step, c).wait_send()

    for k in range(1, dp):
        adapters_copy(k).wait_send()
        share_copy(k).wait_send()
    for kind in range(4):
        for k in range(1, n):
            z_copy(kind, k).wait_send()
    pltpu.make_async_copy(total, grads_ref, grads_sem).wait()
    for t in range(n):
        out_copy(t).wait()


def body(
    n,
    dp,
    output_gradient,
    attention_input,
    output_weight,
    adapter_down_weight,
    adapter_up_weight,
    tenant_of_block,
    slot_of_tenant,
):
    f32, bf16 = jnp.float32, jnp.bfloat16
    blocks = tenant_of_block.shape[0]
    shard_rows, local = attention_input.shape
    own_rows, width = output_gradient.shape
    held, _, rank = adapter_down_weight.shape
    chunks = max(1, own_rows // 32)
    chunk = width // chunks

    adapters = jnp.concatenate([jnp.swapaxes(adapter_down_weight, 1, 2), adapter_up_weight], axis=1)
    dma = pltpu.SemaphoreType.DMA
    smem = pl.BlockSpec(memory_space=pltpu.SMEM)
    vmem = pl.BlockSpec(memory_space=pltpu.VMEM)
    anywhere = pl.BlockSpec(memory_space=pl.ANY)
    grad_in, grads = pl.pallas_call(
        functools.partial(kernel, n, dp, chunks),
        out_shape=(
            jax.ShapeDtypeStruct((shard_rows, local), bf16),
            jax.ShapeDtypeStruct((held, 2 * rank, local), f32),
        ),
        in_specs=[smem, smem, vmem, anywhere, anywhere, anywhere],
        out_specs=(anywhere, anywhere),
        scratch_shapes=[
            pltpu.VMEM((chunks, local, chunk), bf16),
            pltpu.VMEM((n, chunks, own_rows, chunk), bf16),
            pltpu.VMEM((n, own_rows, local), f32),
            pltpu.VMEM((shard_rows, local), bf16),
            pltpu.VMEM((dp * held, 2 * rank, local), bf16),
            pltpu.VMEM((blocks, 2 * rank, local), bf16),
            pltpu.VMEM((n, rank, local), bf16),
            pltpu.VMEM((n, rank, own_rows), f32),
            pltpu.VMEM((n, rank, own_rows), f32),
            pltpu.VMEM((n, rank, own_rows), bf16),
            pltpu.VMEM((n, rank, local), bf16),
            pltpu.VMEM((n, rank, local), bf16),
            pltpu.VMEM((blocks, 2 * rank, local), f32),
            pltpu.VMEM((dp, held, 2 * rank, local), bf16),
            pltpu.VMEM((dp, held, 2 * rank, local), bf16),
            pltpu.VMEM((held, 2 * rank, local), f32),
            pltpu.VMEM((n, own_rows, local), bf16),
            dma((chunks,)),
            dma,
            dma((chunks,)),
            dma((2, n - 1, chunks)),
            dma((2, n - 1, chunks)),
            dma((dp - 1,)),
            dma((dp - 1,)),
            dma((4, n - 1)),
            dma((4, n - 1)),
            dma((dp - 1,)),
            dma((dp - 1,)),
            dma((n,)),
            dma,
        ],
        compiler_params=pltpu.CompilerParams(
            collective_id=0, has_side_effects=True, vmem_limit_bytes=62 * 1024 * 1024
        ),
        cost_estimate=pl.CostEstimate(
            flops=2 * shard_rows * width * local,
            bytes_accessed=2 * local * width,
            transcendentals=0,
        ),
        name="gather_and_multiply",
    )(tenant_of_block, slot_of_tenant, adapters, output_gradient, attention_input, output_weight)
    return grad_in, jnp.swapaxes(grads[:, :rank], 1, 2), grads[:, rank:]


def solution(mesh):
    in_specs = (
        P(("groups", "dp", "tensor"), None),
        P(("groups", "dp"), "tensor"),
        P("tensor", None),
        P("dp", "tensor", None),
        P("dp", None, "tensor"),
        P(("groups", "dp")),
        P(),
    )
    out_specs = (
        P(("groups", "dp"), "tensor"),
        P(("groups", "dp"), "tensor", None),
        P(("groups", "dp"), None, "tensor"),
    )
    sizes = mesh.shape["tensor"], mesh.shape["dp"]

    def per_device(*args):
        return body(*sizes, *args)

    return jax.shard_map(per_device, mesh=mesh, in_specs=in_specs, out_specs=out_specs, check_vma=False)
```
